512 devices in a mesh: replica: 4 (over z_hi), row: 16 (over z_lo, y), col: 8 (over x, core).
Axes of the slice: x: 4, y: 8, z: 8 (z_hi: 4, z_lo: 2; z = z_hi * 2 + z_lo), core: 2. Of those that a mesh axis runs over, the one named last changes fastest.
Arguments:
- hidden: bfloat16 [4, 1408, 14336], P('replica', 'col', 'row'), may hold values from -6 to 6
- cotangent: bfloat16 [4, 1408, 4096], P('replica', 'row', 'col'), may hold values from -6 to 6
- weight: bfloat16 [4, 14336, 4096], P('replica', 'row', 'col'), may hold values from -6 to 6
- prev_weight: bfloat16 [4, 14336, 4096], P('replica', 'row', 'col'), may hold values from -6 to 6
- prev_grad: bfloat16 [4, 14336, 4096], P('replica', 'row', 'col'), may hold values from -3 to 3
Outputs:
- output: bfloat16 [4, 1408, 4096], P('replica', 'row', 'col')
- hidden_grad: bfloat16 [4, 1408, 14336], P('replica', 'col', 'row')
- new_weight: bfloat16 [4, 14336, 4096], P('replica', 'row', 'col')
The draws below stay inside these ranges and needn't reach their ends.
All inputs are finite; a program needn't handle non-finite values.
Results may differ from the reference program's by a relative error of at most 0.017.
Values may be sent and summed in bfloat16 or wider, within the bound.
No kernel may reach another device: no remote copies, remote signals or barrier semaphores. Data moves between devices by JAX's collectives and lax.ppermute only.
A program may use at most 64 MiB of HBM per device.

```python
import jax
import jax.numpy as jnp
from jax import lax

D = 4096
FF = 14336
TOK_GROUP = 1408
N_REPLICA = 4
N_ROW = 16
N_COL = 8


def level_of(stream_key, shape, pieces, smallest, high):
    level, own = 1.0, jax.random.fold_in(stream_key, 6)
    for position, shards_of in pieces:
        draws = jnp.exp(jax.random.uniform(jax.random.fold_in(own, position), (shards_of,), jnp.float32, smallest / len(pieces), high / len(pieces)))
        level = level * jnp.repeat(draws, shape[position] // shards_of).reshape([-1 if axis == position else 1 for axis in range(len(shape))])
    return level


def gaussian(stream_key, dims, width, limit, pieces=(), kind=jnp.bfloat16):
    drawn = jax.random.normal(stream_key, dims, jnp.float32) * width
    if len(pieces) > 0:
        drawn = level_of(stream_key, dims, pieces, -0.22, 0.18) * drawn
    return jnp.clip(drawn, min=-limit, max=limit).astype(kind)


def setup_inputs(seed: int = 0) -> dict:
    key_of = jax.random.split(jax.random.key(seed), 6)
    return {
        "hidden": gaussian(key_of[0], (N_REPLICA, TOK_GROUP, FF), 1.0, 6.0, ((0, 4), (1, 8), (2, 16))),
        "cotangent": gaussian(key_of[1], (N_REPLICA, TOK_GROUP, D), 1.0, 6.0, ((0, 4), (1, 16), (2, 8))),
        "weight": gaussian(key_of[2], (N_REPLICA, FF, D), 1.0, 6.0, ((0, 4), (1, 16), (2, 8))),
        "prev_weight": gaussian(key_of[3], (N_REPLICA, FF, D), 1.0, 6.0, ((0, 4), (1, 16), (2, 8))),
        "prev_grad": gaussian(key_of[4], (N_REPLICA, FF, D), 0.5, 3.0, ((0, 4), (1, 16), (2, 8))),
    }


def reference(hidden, cotangent, weight, prev_weight, prev_grad):
    scale = FF ** -0.5
    row_width = FF // N_ROW
    col_width = D // N_COL

    def blended(index):
        value = weight[index].astype(jnp.float32) - 0.5 * prev_weight[index].astype(jnp.float32)
        return value.astype(jnp.bfloat16).astype(jnp.float32)

    def one_replica(index):
        inputs = hidden[index]
        upstream = cotangent[index]
        matrix = weight[index]

        def forward_block(block, total):
            start = (block * row_width).astype(jnp.int32)
            piece_in = lax.dynamic_slice_in_dim(inputs, start, row_width, 1)
            piece_w = lax.dynamic_slice_in_dim(matrix, start, row_width, 0)
            term = jnp.dot(piece_in, piece_w, preferred_element_type=jnp.float32) * scale
            return total + term.astype(jnp.bfloat16).astype(jnp.float32)

        output = lax.fori_loop(0, N_ROW, forward_block, jnp.zeros((TOK_GROUP, D), jnp.float32)).astype(jnp.bfloat16)

        def backward_block(block, total):
            start = (block * col_width).astype(jnp.int32)
            piece_up = lax.dynamic_slice_in_dim(upstream, start, col_width, 1)
            piece_w = lax.dynamic_slice_in_dim(matrix, start, col_width, 1)
            term = lax.dot_general(piece_up, piece_w, (((1,), (1,)), ((), ())), preferred_element_type=jnp.float32) * scale
            return total + term.astype(jnp.bfloat16).astype(jnp.float32)

        hidden_grad = lax.fori_loop(0, N_COL, backward_block, jnp.zeros((TOK_GROUP, FF), jnp.float32)).astype(jnp.bfloat16)
        grad = lax.dot_general(inputs, upstream, (((0,), (0,)), ((), ())), preferred_element_type=jnp.float32) * scale
        count = jnp.int32(N_REPLICA)
        left = blended(((index - 1) % count).astype(jnp.int32))
        right = blended(((index + 1) % count).astype(jnp.int32))
        centre = blended(index)
        fresh = centre + (left + centre + right) / 3.0 - 0.5 * (grad - prev_grad[index].astype(jnp.float32))
        return output, hidden_grad, fresh.astype(jnp.bfloat16)

    output, hidden_grad, new_weight = lax.map(one_replica, jnp.arange(N_REPLICA, dtype=jnp.int32))
    return (output, hidden_grad, new_weight)
```

```python
import jax
import jax.numpy as jnp
from jax import lax
from jax.experimental import pallas as pl
from jax.experimental.pallas import tpu as pltpu
from jax.sharding import Mesh
from jax.sharding import PartitionSpec as P

FF = 14336
SCALE = FF ** (-0.5)
ROW = ("z", "y")
COL = ("x", "c")
F32 = jnp.float32
BF16 = jnp.bfloat16
PARAMS = pltpu.CompilerParams(vmem_limit_bytes=16 * 2**20)
N_X = 4


def shifted(array, axis, by):
    peers = lax.axis_size(axis)
    return lax.ppermute(array, axis, [(i, (i + by) % peers) for i in range(peers)])


def exchanged(parts, axis):
    return lax.all_to_all(parts, axis, 0, 0, tiled=False)


def dot(a, b, ca, cb):
    return lax.dot_general(a, b, (((ca,), (cb,)), ((), ())), preferred_element_type=F32)


def column(d, other):
    x, c = lax.axis_index("x"), lax.axis_index("c")
    return (x + d) % N_X * 2 + (1 - c if other else c)


def fan_kernel(u, u_z, out):
    for y in range(out.shape[0]):
        out[y, 0] = u[...]
        out[y, 1] = u_z[...]


def fan(u, u_z):
    return pl.pallas_call(
        fan_kernel,
        out_shape=jax.ShapeDtypeStruct((2 * N_X, 2, *u.shape), u.dtype),
        compiler_params=PARAMS,
        name="fan",
    )(u, u_z)


def forward_kernel(*refs):
    blocks, (w, out) = refs[:-2], refs[-2:]
    rows = out.shape[1]
    for k, block in enumerate(blocks):
        at = column(k % N_X, k >= N_X)
        term = dot(block[...], w[...], 1, 0) * SCALE
        out[2 * at] = term[:rows].astype(BF16)
        out[2 * at + 1] = term[rows:].astype(BF16)


def forward(blocks, w, rows):
    return pl.pallas_call(
        forward_kernel,
        out_shape=jax.ShapeDtypeStruct((4 * N_X, rows, w.shape[1]), BF16),
        compiler_params=PARAMS,
        name="forward",
    )(*blocks, w)


def backward_kernel(u, w, send, keep, ordered):
    for other in (1, 0):
        for d in range(N_X):
            at = column(d, other)
            y, far = 2 * at % (2 * N_X), (at // N_X + lax.axis_index("z")) % 2
            pair = [u[y + j, far].astype(F32) for j in range(2)]
            both = jnp.concatenate(pair).astype(BF16)
            ordered[other * N_X + d] = both
            term = dot(both, w[...], 1, 1) * SCALE
            (send if other else keep)[d] = term.astype(BF16)


def backward(u, w):
    rows, feats = u.shape[2:]
    half = jax.ShapeDtypeStruct((N_X, 2 * rows, w.shape[0]), BF16)
    return pl.pallas_call(
        backward_kernel,
        out_shape=[half, half, jax.ShapeDtypeStruct((2 * N_X, 2 * rows, feats), BF16)],
        compiler_params=PARAMS,
        name="backward",
    )(u, w)


def step_kernel(*refs):
    blocks, (u, blend, prev, out) = refs[:-4], refs[-4:]
    h = jnp.concatenate([block[...] for block in blocks])
    grad = dot(h, u[...], 0, 0)
    out[...] = blend[...].astype(F32) * (4.0 / 3.0) - 0.5 * (
        grad * SCALE - prev[...].astype(F32)
    )


def local_step(blocks, u, blend, prev):
    units, feats = blend.shape
    h_spec = pl.BlockSpec((blocks[0].shape[0], 128), lambda i: (0, i))
    w_spec = pl.BlockSpec((128, feats), lambda i: (i, 0))
    return pl.pallas_call(
        step_kernel,
        grid=(units // 128,),
        out_shape=jax.ShapeDtypeStruct((units, feats), F32),
        in_specs=[h_spec] * len(blocks) + [pl.BlockSpec(u.shape, lambda i: (0, 0)), w_spec, w_spec],
        out_specs=w_spec,
        compiler_params=PARAMS,
        name="step",
    )(*blocks, u, blend, prev)


def on_device(hidden, cotangent, weight, prev_weight, prev_grad):
    tok, units = hidden.shape[1:]
    rows, feats = cotangent.shape[1:]
    h, u, w = hidden[0], cotangent[0], weight[0]

    blend = (w.astype(F32) - 0.5 * prev_weight[0].astype(F32)).astype(BF16)
    cut = units * 3 // 8
    left = [shifted(blend[:cut], "replica", 1), shifted(blend[cut:], "replica", 1)]
    right = [shifted(blend[:cut], "replica", -1), shifted(blend[cut:], "replica", -1)]

    u_all = exchanged(fan(u, shifted(u, "z", 1)), "y")

    blocks = [h, shifted(h, "x", -1), shifted(h, "x", 2), shifted(h, "x", 1)]
    blocks += [shifted(block, "c", 1) for block in blocks]

    o = forward(blocks, w, rows)
    left[0], right[0], o = lax.optimization_barrier((left[0], right[0], o))
    o = exchanged(o, ROW)
    output = o.astype(F32).sum(axis=0).astype(BF16)

    b_send, b_keep, u_rel = backward(u_all, w)
    b = shifted(b_send, "c", 1).astype(F32) + b_keep.astype(F32)
    got = [shifted(b[d].astype(BF16), "x", d) for d in range(1, N_X)]
    left[1], right[1], *got = lax.optimization_barrier((left[1], right[1], *got))
    hidden_grad = b[0] + sum(part.astype(F32) for part in got)

    base = local_step(blocks, u_rel.reshape(2 * N_X * tok, feats), blend, prev_grad[0])
    around = jnp.concatenate([a.astype(F32) + b.astype(F32) for a, b in zip(left, right)])
    fresh = (base + around / 3.0).astype(BF16)
    return output[None], hidden_grad.astype(BF16)[None], fresh[None]


def solution(mesh):
    torus = Mesh(
        mesh.devices.reshape(mesh.shape["replica"], 2, 8, N_X, 2),
        ("replica", "z", "y", "x", "c"),
    )
    return jax.shard_map(
        on_device,
        mesh=torus,
        in_specs=(
            P("replica", COL, ROW),
            P("replica", ROW, COL),
            P("replica", ROW, COL),
            P("replica", ROW, COL),
            P("replica", ROW, COL),
        ),
        out_specs=(P("replica", ROW, COL), P("replica", COL, ROW), P("replica", ROW, COL)),
        check_vma=False,
    )
```

```python
import jax
import jax.numpy as jnp
from jax import lax
from jax.experimental import pallas as pl
from jax.experimental.pallas import tpu as pltpu
from jax.sharding import Mesh
from jax.sharding import PartitionSpec as P

FF = 14336
SCALE = FF ** (-0.5)
ROW = ("z", "y")
COL = ("x", "c")
F32 = jnp.float32
BF16 = jnp.bfloat16
PARAMS = pltpu.CompilerParams(vmem_limit_bytes=16 * 2**20)
N_X = 4


def shifted(array, axis, by):
    peers = lax.axis_size(axis)
    return lax.ppermute(array, axis, [(i, (i + by) % peers) for i in range(peers)])


def exchanged(parts, axis):
    return lax.all_to_all(parts, axis, 0, 0, tiled=False)


def dot(a, b, ca, cb):
    return lax.dot_general(a, b, (((ca,), (cb,)), ((), ())), preferred_element_type=F32)


def column(d, other):
    x, c = lax.axis_index("x"), lax.axis_index("c")
    return (x + d) % N_X * 2 + (1 - c if other else c)


def pack_kernel(*refs):
    for k, ref in enumerate(refs[:-1]):
        refs[-1][k] = ref[...]


def pack(*arrays):
    return pl.pallas_call(
        pack_kernel,
        out_shape=jax.ShapeDtypeStruct((len(arrays), *arrays[0].shape), BF16),
        compiler_params=PARAMS,
        name="pack",
    )(*arrays)


def fan_kernel(u, u_z, out):
    for y in range(out.shape[0]):
        out[y, 0] = u[...]
        out[y, 1] = u_z[...]


def fan(u, u_z):
    return pl.pallas_call(
        fan_kernel,
        out_shape=pltpu.HBM((2 * N_X, 2, *u.shape), BF16),
        compiler_params=PARAMS,
        name="fan",
    )(u, u_z)


def whole(refs):
    own, far, oth, oth_far = refs
    return [own[...], *(far[k] for k in range(N_X - 1))] + [
        oth[...],
        *(oth_far[k] for k in range(N_X - 1)),
    ]


def forward_kernel(*refs):
    h, (w, out) = refs[:-2], refs[-2:]
    rows = out.shape[1]
    for k, block in enumerate(whole(h)):
        at = column(k % N_X, k >= N_X)
        term = dot(block, w[...], 1, 0) * SCALE
        out[2 * at] = term[:rows].astype(BF16)
        out[2 * at + 1] = term[rows:].astype(BF16)


def forward(h, w, rows):
    return pl.pallas_call(
        forward_kernel,
        out_shape=pltpu.HBM((4 * N_X, rows, w.shape[1]), BF16),
        compiler_params=PARAMS,
        name="forward",
    )(*h, w)


def backward_kernel(u, w, send, keep, ordered):
    for other in (1, 0):
        for d in range(N_X):
            at = column(d, other)
            y, far = 2 * at % (2 * N_X), (at // N_X + lax.axis_index("z")) % 2
            pair = [u[y + j, far].astype(F32) for j in range(2)]
            both = jnp.concatenate(pair).astype(BF16)
            ordered[other * N_X + d] = both
            term = dot(both, w[...], 1, 1) * SCALE
            (send if other else keep)[d] = term.astype(BF16)


def backward(u, w):
    rows, feats = u.shape[2:]
    half = pltpu.HBM((N_X, 2 * rows, w.shape[0]), BF16)
    return pl.pallas_call(
        backward_kernel,
        out_shape=[half, half, pltpu.HBM((2 * N_X, 2 * rows, feats), BF16)],
        compiler_params=PARAMS,
        name="backward",
    )(u, w)


def merge_kernel(got, keep, own, *outs):
    for d, out in enumerate((own, *outs)):
        out[...] = (got[d].astype(F32) + keep[d].astype(F32)).astype(out.dtype)


def merge(got, keep):
    one = got.shape[1:]
    return pl.pallas_call(
        merge_kernel,
        out_shape=[jax.ShapeDtypeStruct(one, F32)] + [jax.ShapeDtypeStruct(one, BF16)] * (N_X - 1),
        compiler_params=PARAMS,
        name="merge",
    )(got, keep)


def step_kernel(*refs):
    h, (u, blend, prev, left, right, out) = refs[:-6], refs[-6:]
    grad = dot(jnp.concatenate(whole(h)), u[...], 0, 0) * SCALE
    centre = blend[...].astype(F32)
    around = left[...].astype(F32) + centre + right[...].astype(F32)
    fresh = centre + around * (1.0 / 3.0) - 0.5 * (grad - prev[...].astype(F32))
    out[...] = fresh.astype(BF16)


def local_step(h, u, *weights):
    units, feats = weights[0].shape
    tok = h[0].shape[0]
    one = pl.BlockSpec((tok, 128), lambda i: (0, i))
    far = pl.BlockSpec((N_X - 1, tok, 128), lambda i: (0, 0, i))
    w_spec = pl.BlockSpec((128, feats), lambda i: (i, 0))
    u_spec = pl.BlockSpec(u.shape, lambda i: (0, 0))
    return pl.pallas_call(
        step_kernel,
        grid=(units // 128,),
        out_shape=jax.ShapeDtypeStruct((units, feats), BF16),
        in_specs=[one, far, one, far, u_spec] + [w_spec] * len(weights),
        out_specs=w_spec,
        compiler_params=PARAMS,
        name="step",
    )(*h, u, *weights)


def gather(h, u, u_z, w):
    far = pack(*(shifted(h, "x", -d) for d in range(1, N_X)))
    acts = (far, shifted(h, "c", 1), shifted(far, "c", 1))
    u_all = exchanged(fan(u, u_z), "y")
    return forward((h, *acts), w, u.shape[0]), u_all, *acts


def on_device(hidden, cotangent, weight, prev_weight, prev_grad):
    tok = hidden.shape[1]
    h, u, w = hidden[0], cotangent[0], weight[0]

    u_z = shifted(u, "z", 1)
    blend = (w.astype(F32) - 0.5 * prev_weight[0].astype(F32)).astype(BF16)
    blend, u_z = lax.optimization_barrier((blend, u_z))
    left, right = shifted(blend, "replica", 1), shifted(blend, "replica", -1)

    o, u_all, *acts = lax.cond(u[0, 0] == u[0, 0], gather, gather, h, u, u_z, w)
    left, right, o, u_all = lax.optimization_barrier((left, right, o, u_all))

    o = exchanged(o, ROW)
    output = o.astype(F32).sum(axis=0).astype(BF16)

    b_send, b_keep, u_rel = backward(u_all, w)
    b_own, *b_far = merge(shifted(b_send, "c", 1), b_keep)
    got = [shifted(part, "x", d) for d, part in enumerate(b_far, 1)]
    hidden_grad = (b_own + sum(part.astype(F32) for part in got)).astype(BF16)

    u_rel = u_rel.reshape(2 * N_X * tok, u.shape[1])
    fresh = local_step((h, *acts), u_rel, blend, prev_grad[0], left, right)
    return output[None], hidden_grad[None], fresh[None]


def solution(mesh):
    torus = Mesh(
        mesh.devices.reshape(mesh.shape["replica"], 2, 8, N_X, 2),
        ("replica", "z", "y", "x", "c"),
    )
    return jax.shard_map(
        on_device,
        mesh=torus,
        in_specs=(
            P("replica", COL, ROW),
            P("replica", ROW, COL),
            P("replica", ROW, COL),
            P("replica", ROW, COL),
            P("replica", ROW, COL),
        ),
        out_specs=(P("replica", ROW, COL), P("replica", COL, ROW), P("replica", ROW, COL)),
        check_vma=False,
    )
```

```python
import jax
import jax.numpy as jnp
from jax import lax
from jax.experimental import pallas as pl
from jax.experimental.pallas import tpu as pltpu
from jax.sharding import Mesh
from jax.sharding import PartitionSpec as P

FF = 14336
SCALE = FF ** (-0.5)
ROW = ("z", "y")
COL = ("x", "c")
F32 = jnp.float32
BF16 = jnp.bfloat16
PARAMS = pltpu.CompilerParams(vmem_limit_bytes=16 * 2**20)
N_X = 4


def shifted(array, axis, by):
    peers = lax.axis_size(axis)
    return lax.ppermute(array, axis, [(i, (i + by) % peers) for i in range(peers)])


def exchanged(parts, axis):
    return lax.all_to_all(parts, axis, 0, 0, tiled=False)


def dot(a, b, ca, cb):
    return lax.dot_general(a, b, (((ca,), (cb,)), ((), ())), preferred_element_type=F32)


def column(d, other):
    x, c = lax.axis_index("x"), lax.axis_index("c")
    return (x + d) % N_X * 2 + (1 - c if other else c)


def pack_kernel(*refs):
    for k, ref in enumerate(refs[:-1]):
        refs[-1][k] = ref[...]


def pack(*arrays):
    return pl.pallas_call(
        pack_kernel,
        out_shape=jax.ShapeDtypeStruct((len(arrays), *arrays[0].shape), BF16),
        compiler_params=PARAMS,
        name="pack",
    )(*arrays)


def fan_kernel(u, u_z, out):
    for y in range(out.shape[0]):
        out[y, 0] = u[...]
        out[y, 1] = u_z[...]


def fan(u, u_z):
    return pl.pallas_call(
        fan_kernel,
        out_shape=pltpu.HBM((2 * N_X, 2, *u.shape), BF16),
        compiler_params=PARAMS,
        name="fan",
    )(u, u_z)


def whole(refs):
    own, far, oth, oth_far = refs
    return [own[...], *(far[k] for k in range(N_X - 1))] + [
        oth[...],
        *(oth_far[k] for k in range(N_X - 1)),
    ]


def forward_kernel(*refs):
    h, (w, out) = refs[:-2], refs[-2:]
    rows = out.shape[1]
    for k, block in enumerate(whole(h)):
        at = column(k % N_X, k >= N_X)
        term = dot(block, w[...], 1, 0) * SCALE
        out[2 * at] = term[:rows].astype(BF16)
        out[2 * at + 1] = term[rows:].astype(BF16)


def forward(h, w, rows):
    return pl.pallas_call(
        forward_kernel,
        out_shape=pltpu.HBM((4 * N_X, rows, w.shape[1]), BF16),
        compiler_params=PARAMS,
        name="forward",
    )(*h, w)


def backward_kernel(u, w, send, keep, ordered):
    for other in (1, 0):
        for d in range(N_X):
            at = column(d, other)
            y, far = 2 * at % (2 * N_X), (at // N_X + lax.axis_index("z")) % 2
            pair = [u[y + j, far].astype(F32) for j in range(2)]
            both = jnp.concatenate(pair).astype(BF16)
            ordered[other * N_X + d] = both
            term = dot(both, w[...], 1, 1) * SCALE
            (send if other else keep)[d] = term.astype(BF16)


def backward(u, w):
    rows, feats = u.shape[2:]
    half = pltpu.HBM((N_X, 2 * rows, w.shape[0]), BF16)
    return pl.pallas_call(
        backward_kernel,
        out_shape=[half, half, pltpu.HBM((2 * N_X, 2 * rows, feats), BF16)],
        compiler_params=PARAMS,
        name="backward",
    )(u, w)


def merge_kernel(got, keep, own, *outs):
    for d, out in enumerate((own, *outs)):
        out[...] = (got[d].astype(F32) + keep[d].astype(F32)).astype(out.dtype)


def merge(got, keep):
    one = got.shape[1:]
    return pl.pallas_call(
        merge_kernel,
        out_shape=[jax.ShapeDtypeStruct(one, F32)] + [jax.ShapeDtypeStruct(one, BF16)] * (N_X - 1),
        compiler_params=PARAMS,
        name="merge",
    )(got, keep)


def step_kernel(*refs):
    h, (u, blend, prev, left, right, out) = refs[:-6], refs[-6:]
    grad = dot(jnp.concatenate(whole(h)), u[...], 0, 0) * SCALE
    centre = blend[...].astype(F32)
    around = left[...].astype(F32) + centre + right[...].astype(F32)
    fresh = centre + around * (1.0 / 3.0) - 0.5 * (grad - prev[...].astype(F32))
    out[...] = fresh.astype(BF16)


def local_step(h, u, *weights):
    units, feats = weights[0].shape
    tok = h[0].shape[0]
    one = pl.BlockSpec((tok, 128), lambda i: (0, i))
    far = pl.BlockSpec((N_X - 1, tok, 128), lambda i: (0, 0, i))
    w_spec = pl.BlockSpec((128, feats), lambda i: (i, 0))
    u_spec = pl.BlockSpec(u.shape, lambda i: (0, 0))
    return pl.pallas_call(
        step_kernel,
        grid=(units // 128,),
        out_shape=jax.ShapeDtypeStruct((units, feats), BF16),
        in_specs=[one, far, one, far, u_spec] + [w_spec] * len(weights),
        out_specs=w_spec,
        compiler_params=PARAMS,
        name="step",
    )(*h, u, *weights)


def total_kernel(parts, out):
    whole_sum = parts[0].astype(F32)
    for k in range(1, parts.shape[0]):
        whole_sum += parts[k].astype(F32)
    out[...] = whole_sum.astype(BF16)


def total(parts):
    return pl.pallas_call(
        total_kernel,
        out_shape=jax.ShapeDtypeStruct(parts.shape[1:], BF16),
        compiler_params=PARAMS,
        name="total",
    )(parts)


def gather(h, u, u_z, w):
    far = pack(*(shifted(h, "x", -d) for d in range(1, N_X)))
    acts = (far, shifted(h, "c", 1), shifted(far, "c", 1))
    u_all = exchanged(fan(u, u_z), "y")
    return forward((h, *acts), w, u.shape[0]), u_all, *acts


def on_device(hidden, cotangent, weight, prev_weight, prev_grad):
    tok = hidden.shape[1]
    h, u, w = hidden[0], cotangent[0], weight[0]

    u_z = shifted(u, "z", 1)
    blend = (w.astype(F32) - 0.5 * prev_weight[0].astype(F32)).astype(BF16)
    pick = u[0, 0] == u[0, 0]
    blend, u_z, pick = lax.optimization_barrier((blend, u_z, pick))
    left, right = shifted(blend, "replica", 1), shifted(blend, "replica", -1)

    o, u_all, *acts = lax.cond(pick, gather, gather, h, u, u_z, w)
    left, right, o, u_all = lax.optimization_barrier((left, right, o, u_all))

    o = exchanged(o, ROW)
    output = total(o)

    b_send, b_keep, u_rel = backward(u_all, w)
    b_own, *b_far = merge(shifted(b_send, "c", 1), b_keep)
    got = [shifted(part, "x", d) for d, part in enumerate(b_far, 1)]
    hidden_grad = (b_own + sum(part.astype(F32) for part in got)).astype(BF16)

    u_rel = u_rel.reshape(2 * N_X * tok, u.shape[1])
    fresh = local_step((h, *acts), u_rel, blend, prev_grad[0], left, right)
    return output[None], hidden_grad[None], fresh[None]


def solution(mesh):
    torus = Mesh(
        mesh.devices.reshape(mesh.shape["replica"], 2, 8, N_X, 2),
        ("replica", "z", "y", "x", "c"),
    )
    return jax.shard_map(
        on_device,
        mesh=torus,
        in_specs=(
            P("replica", COL, ROW),
            P("replica", ROW, COL),
            P("replica", ROW, COL),
            P("replica", ROW, COL),
            P("replica", ROW, COL),
        ),
        out_specs=(P("replica", ROW, COL), P("replica", COL, ROW), P("replica", ROW, COL)),
        check_vma=False,
    )
```

```python
import jax
import jax.numpy as jnp
from jax import lax
from jax.experimental import pallas as pl
from jax.experimental.pallas import tpu as pltpu
from jax.sharding import Mesh
from jax.sharding import PartitionSpec as P

FF = 14336
SCALE = FF ** (-0.5)
ROW = ("z", "y")
COL = ("x", "c")
F32 = jnp.float32
BF16 = jnp.bfloat16
PARAMS = pltpu.CompilerParams(vmem_limit_bytes=16 * 2**20)
N_X = 4


def shifted(array, axis, by):
    peers = lax.axis_size(axis)
    return lax.ppermute(array, axis, [(i, (i + by) % peers) for i in range(peers)])


def exchanged(parts, axis):
    return lax.all_to_all(parts, axis, 0, 0, tiled=False)


def dot(a, b, ca, cb):
    return lax.dot_general(a, b, (((ca,), (cb,)), ((), ())), preferred_element_type=F32)


def column(d, other):
    x, c = lax.axis_index("x"), lax.axis_index("c")
    return (x + d) % N_X * 2 + (1 - c if other else c)


def pack_kernel(*refs):
    for k, ref in enumerate(refs[:-1]):
        refs[-1][k] = ref[...]


def pack(*arrays):
    return pl.pallas_call(
        pack_kernel,
        out_shape=jax.ShapeDtypeStruct((len(arrays), *arrays[0].shape), BF16),
        compiler_params=PARAMS,
        name="pack",
    )(*arrays)


def fan_kernel(u, u_z, out):
    for y in range(out.shape[0]):
        out[y, 0] = u[...]
        out[y, 1] = u_z[...]


def fan(u, u_z):
    return pl.pallas_call(
        fan_kernel,
        out_shape=pltpu.HBM((2 * N_X, 2, *u.shape), BF16),
        compiler_params=PARAMS,
        name="fan",
    )(u, u_z)


def whole(refs):
    own, far, oth, oth_far = refs
    return [own[...], *(far[k] for k in range(N_X - 1))] + [
        oth[...],
        *(oth_far[k] for k in range(N_X - 1)),
    ]


def forward_kernel(*refs):
    h, (w, out) = refs[:-2], refs[-2:]
    rows = out.shape[1]
    for k, block in enumerate(whole(h)):
        at = column(k % N_X, k >= N_X)
        term = dot(block, w[...], 1, 0) * SCALE
        out[2 * at] = term[:rows].astype(BF16)
        out[2 * at + 1] = term[rows:].astype(BF16)


def forward(h, w, rows):
    return pl.pallas_call(
        forward_kernel,
        out_shape=pltpu.HBM((4 * N_X, rows, w.shape[1]), BF16),
        compiler_params=PARAMS,
        name="forward",
    )(*h, w)


def backward_kernel(u, w, send, keep, ordered):
    for other in (1, 0):
        for d in range(N_X):
            at = column(d, other)
            y, far = 2 * at % (2 * N_X), (at // N_X + lax.axis_index("z")) % 2
            pair = [u[y + j, far].astype(F32) for j in range(2)]
            both = jnp.concatenate(pair).astype(BF16)
            ordered[other * N_X + d] = both
            term = dot(both, w[...], 1, 1) * SCALE
            (send if other else keep)[d] = term.astype(BF16)


def backward(u, w):
    rows, feats = u.shape[2:]
    half = pltpu.HBM((N_X, 2 * rows, w.shape[0]), BF16)
    return pl.pallas_call(
        backward_kernel,
        out_shape=[jax.ShapeDtypeStruct(half.shape, BF16), half, pltpu.HBM((2 * N_X, 2 * rows, feats), BF16)],
        compiler_params=PARAMS,
        name="backward",
    )(u, w)


def merge_kernel(got, keep, own, *outs):
    for d, out in enumerate((own, *outs)):
        out[...] = (got[d].astype(F32) + keep[d].astype(F32)).astype(out.dtype)


def merge(got, keep):
    one = got.shape[1:]
    return pl.pallas_call(
        merge_kernel,
        out_shape=[jax.ShapeDtypeStruct(one, F32)] + [jax.ShapeDtypeStruct(one, BF16)] * (N_X - 1),
        compiler_params=PARAMS,
        name="merge",
    )(got, keep)


def step_kernel(*refs):
    h, (u, blend, prev, left, right, out) = refs[:-6], refs[-6:]
    grad = dot(jnp.concatenate(whole(h)), u[...], 0, 0) * SCALE
    centre = blend[...].astype(F32)
    around = left[...].astype(F32) + centre + right[...].astype(F32)
    fresh = centre + around * (1.0 / 3.0) - 0.5 * (grad - prev[...].astype(F32))
    out[...] = fresh.astype(BF16)


def local_step(h, u, *weights):
    units, feats = weights[0].shape
    tok = h[0].shape[0]
    one = pl.BlockSpec((tok, 128), lambda i: (0, i))
    far = pl.BlockSpec((N_X - 1, tok, 128), lambda i: (0, 0, i))
    w_spec = pl.BlockSpec((128, feats), lambda i: (i, 0))
    u_spec = pl.BlockSpec(u.shape, lambda i: (0, 0))
    return pl.pallas_call(
        step_kernel,
        grid=(units // 128,),
        out_shape=jax.ShapeDtypeStruct((units, feats), BF16),
        in_specs=[one, far, one, far, u_spec] + [w_spec] * len(weights),
        out_specs=w_spec,
        compiler_params=PARAMS,
        name="step",
    )(*h, u, *weights)


def total_kernel(parts, out):
    whole_sum = parts[0].astype(F32)
    for k in range(1, parts.shape[0]):
        whole_sum += parts[k].astype(F32)
    out[...] = whole_sum.astype(BF16)


def total(parts):
    return pl.pallas_call(
        total_kernel,
        out_shape=jax.ShapeDtypeStruct(parts.shape[1:], BF16),
        compiler_params=PARAMS,
        name="total",
    )(parts)


def gather(h, u, u_z, w):
    far = pack(*(shifted(h, "x", -d) for d in range(1, N_X)))
    acts = (far, shifted(h, "c", 1), shifted(far, "c", 1))
    u_all = exchanged(fan(u, u_z), "y")
    return forward((h, *acts), w, u.shape[0]), u_all, *acts


def on_device(hidden, cotangent, weight, prev_weight, prev_grad):
    tok = hidden.shape[1]
    h, u, w = hidden[0], cotangent[0], weight[0]

    u_z = shifted(u, "z", 1)
    blend = (w.astype(F32) - 0.5 * prev_weight[0].astype(F32)).astype(BF16)
    pick = u[0, 0] == u[0, 0]
    blend, u_z, pick = lax.optimization_barrier((blend, u_z, pick))
    left, right = shifted(blend, "replica", 1), shifted(blend, "replica", -1)

    o, u_all, *acts = lax.cond(pick, gather, gather, h, u, u_z, w)
    left, right, o, u_all = lax.optimization_barrier((left, right, o, u_all))

    o = exchanged(o, ROW)
    output = total(o)

    b_send, b_keep, u_rel = backward(u_all, w)
    b_own, *b_far = merge(shifted(b_send, "c", 1), b_keep)
    got = [shifted(part, "x", d) for d, part in enumerate(b_far, 1)]
    hidden_grad = (b_own + sum(part.astype(F32) for part in got)).astype(BF16)

    u_rel = u_rel.reshape(2 * N_X * tok, u.shape[1])
    fresh = local_step((h, *acts), u_rel, blend, prev_grad[0], left, right)
    return output[None], hidden_grad[None], fresh[None]


def solution(mesh):
    torus = Mesh(
        mesh.devices.reshape(mesh.shape["replica"], 2, 8, N_X, 2),
        ("replica", "z", "y", "x", "c"),
    )
    return jax.shard_map(
        on_device,
        mesh=torus,
        in_specs=(
            P("replica", COL, ROW),
            P("replica", ROW, COL),
            P("replica", ROW, COL),
            P("replica", ROW, COL),
            P("replica", ROW, COL),
        ),
        out_specs=(P("replica", ROW, COL), P("replica", COL, ROW), P("replica", ROW, COL)),
        check_vma=False,
    )
```
